32 devices in a mesh: group: 2 (over x), expert: 8 (over z, y), dp: 2 (over core).
Axes of the slice: x: 2, y: 2, z: 4, core: 2. Of those that a mesh axis runs over, the one named last changes fastest.
Arguments:
- tokens: bfloat16 [4096, 4096], P(('group', 'expert', 'dp')), parts along dimension 0, may hold values from -6 to 6
- out_grad: bfloat16 [4096, 4096], P(('group', 'expert', 'dp')), parts along dimension 0, may hold values from -6 to 6
- routes: int32 [4096, 2], P('group'), parts along dimension 0, may hold values from 0 to 3, all different within a row
- route_weight: float32 [4096, 2], P('group'), parts along dimension 0, may hold values from 0.1 to 0.9
- gate_pre: bfloat16 [8, 1536, 3584], P('expert', ('group', 'dp')), parts along dimension 1, may hold values from -6 to 6
- up_pre: bfloat16 [8, 1536, 3584], P('expert', ('group', 'dp')), parts along dimension 1, may hold values from -6 to 6
- hid_grad: bfloat16 [8, 1536, 3584], P('expert', ('group', 'dp')), parts along dimension 1, may hold values from -6 to 6
- proj_model: bfloat16 [4096, 64], replicated, may hold values from -0.09375 to 0.09375
- proj_hidden: bfloat16 [7168, 64], replicated, may hold values from -0.0625 to 0.0625
- val_sketch: bfloat16 [128, 49152], P('dp', 'expert'), may hold values from -0.00390625 to 0.00390625
Outputs:
- influence: float32 [4, 128], P('group', 'dp'), parts along dimension 0
The draws below stay inside these ranges and needn't reach their ends.
There are 2 independent parts, one for each index of `group`. The reference program is written for one: setup_inputs(seed, part) draws one part's arguments, and reference() takes and returns one part's arrays. A program takes and returns all parts, laid end to end along the dimension named above; an argument that names none is the same for every part. Nothing has to cross between parts.
Inputs may be any that keep to these rules, and one draw needn't show every extreme that they name: `routes`: the two experts of a row differ; every expert is named by some row.
All inputs are finite; a program needn't handle non-finite values.
Results may differ from the reference program's by a relative error of at most 0.0055.
Values may be sent and summed in bfloat16 or wider, within the bound.
A program may use at most 128 MiB of HBM per device.

```python
import jax
import jax.numpy as jnp
from jax import lax

D = 4096
FW = 7168
K = 64
HALVES = 2
EX_DP = 1
SEQ_DEV = 128
VAL = 128
EXPERTS = 4
SOURCES = 8
EX_SPLIT = 2
NEX = 2
TOK_DEV = 128
TOKENS = 2048
CAP = 48
FC = 3584
SKETCH = 12288
ROWS_E = 768


def level_of(rng, shape, split, least, high):
    def one(position, blocks):
        draws = jax.random.uniform(jax.random.fold_in(jax.random.fold_in(rng, 6), position), (blocks,), jnp.float32, least / len(split), high / len(split))
        return jnp.repeat(jnp.exp(draws), shape[position] // blocks).reshape((-1,) + (1,) * (len(shape) - position - 1))

    loudness = one(*split[0])
    for cut in split[1:]:
        loudness = loudness * one(*cut)
    return loudness


def picks_of(key, rows, count, top, lift):
    ranking = jax.random.permutation(jax.random.fold_in(key, 1), count)
    pull = ranking
    for power in range(3):
        pull = pull * pull // count
    pull = pull * lift // count
    tickets = jax.random.randint(jax.random.fold_in(key, 2), (rows, count), 0, 4096) + pull
    sure = jax.random.permutation(jax.random.fold_in(key, 3), rows)[jnp.arange(count) % rows]
    tickets = jnp.where(jnp.arange(rows)[:, None] == sure[None, :], 1 << 14, tickets)
    merit = tickets * count + jnp.arange(count)
    return lax.top_k(merit.astype(jnp.int32), top)[1].astype(jnp.int32)


def noise(own_key, dims, scale, bound, cuts=(), kind=jnp.bfloat16):
    values = jax.random.normal(own_key, dims, jnp.float32) * scale
    if len(cuts) > 0:
        values = level_of(own_key, dims, cuts, -0.22, 0.18) * values
    return jnp.clip(values, min=-bound, max=bound).astype(kind)


def setup_inputs(seed: int = 0, part: int = 0) -> dict:
    keys = jax.random.split(jax.random.key(seed), 11)
    part_splits = jax.random.split(jax.random.fold_in(keys[10], part), 11)
    return {
        "tokens": noise(part_splits[0], (TOKENS, D), 1.0, 6.0, ((0, 16),)),
        "out_grad": noise(part_splits[1], (TOKENS, D), 1.0, 6.0, ((0, 16),)),
        "routes": picks_of(part_splits[2], TOKENS, EXPERTS, 2, 8192),
        "route_weight": jnp.clip(jax.random.uniform(part_splits[3], (TOKENS, 2), jnp.float32, 0.1, 0.9), 0.1, 0.9),
        "gate_pre": noise(part_splits[4], (EXPERTS * HALVES, ROWS_E, FC), 1.0, 6.0, ((0, 8), (1, 2))),
        "up_pre": noise(part_splits[5], (EXPERTS * HALVES, ROWS_E, FC), 1.0, 6.0, ((0, 8), (1, 2))),
        "hid_grad": noise(part_splits[6], (EXPERTS * HALVES, ROWS_E, FC), 1.0, 6.0, ((0, 8), (1, 2))),
        "proj_model": noise(keys[7], (D, K), D ** -0.5, 0.09375),
        "proj_hidden": noise(keys[8], (FW, K), FW ** -0.5, 0.0625),
        "val_sketch": noise(keys[9], (VAL, EXPERTS * SKETCH), (1.0 / (K * 24)), 0.00390625, ((0, 2), (1, 8))),
    }


def slot_ranks(block_routes, experts):
    labels = jnp.arange(experts, dtype=jnp.int32)
    onehot = (block_routes[..., None] == labels).astype(jnp.int32)
    before = jnp.cumsum(onehot, axis=-2) - onehot
    return jnp.sum(before * onehot, axis=-1)


def swiglu_back(gate_pre, up_pre, hid_grad):
    gate_vals = gate_pre.astype(jnp.float32)
    up_vals = up_pre.astype(jnp.float32)
    grad_vals = hid_grad.astype(jnp.float32)
    gate_sig = jax.nn.sigmoid(gate_vals)
    silu_vals = gate_vals * gate_sig
    hidden = (silu_vals * up_vals).astype(jnp.bfloat16)
    grad_gate = (grad_vals * up_vals * gate_sig * (1.0 + gate_vals * (1.0 - gate_sig))).astype(jnp.bfloat16)
    grad_up = (grad_vals * silu_vals).astype(jnp.bfloat16)
    return hidden, grad_gate, grad_up


def reference(tokens, out_grad, routes, route_weight, gate_pre, up_pre, hid_grad, proj_model, proj_hidden, val_sketch):
    pair_count = 2 * TOK_DEV
    proj_tokens = jnp.dot(tokens, proj_model, preferred_element_type=jnp.float32).astype(jnp.bfloat16)
    grads_full = jnp.dot(out_grad, proj_model, preferred_element_type=jnp.float32)
    scaled_grads = (route_weight.reshape(-1, 1) * jnp.repeat(grads_full, 2, axis=0)).astype(jnp.bfloat16)
    pair_tokens = jnp.repeat(proj_tokens, 2, axis=0)
    route_grid = routes.reshape(SOURCES, EX_SPLIT, pair_count)
    slot_rank = slot_ranks(route_grid, EXPERTS)
    slot_ids = jnp.arange(CAP, dtype=jnp.int32)
    pair_ids = jnp.arange(pair_count, dtype=jnp.int32)
    block_ids = (jnp.arange(SOURCES, dtype=jnp.int32)[:, None] * EX_SPLIT + jnp.arange(EX_SPLIT, dtype=jnp.int32)[None, :])[:, :, None]
    half_ids = jnp.arange(EX_SPLIT, dtype=jnp.int32)[None, :, None]
    example_ids = jnp.arange(NEX, dtype=jnp.int32)

    def one_column(column):
        own_expert = column // HALVES
        column_half = column % HALVES
        matched = ((route_grid == own_expert)[:, :, None, :] & (slot_rank[:, :, None, :] == slot_ids[None, None, :, None])).astype(jnp.int32)
        pair_index = jnp.sum(matched * pair_ids, axis=-1)
        filled = jnp.sum(matched, axis=-1)
        global_pair = jnp.transpose(block_ids * pair_count + pair_index, (1, 0, 2)).reshape(-1)
        example = jnp.transpose(half_ids * EX_DP + (pair_index // 2) // SEQ_DEV, (1, 0, 2)).reshape(-1)
        live_rows = jnp.transpose(filled, (1, 0, 2)).reshape(-1)
        member = ((example[:, None] == example_ids[None, :]) & (live_rows[:, None] > 0)).astype(jnp.float32)
        slot_inputs = pair_tokens[global_pair].astype(jnp.float32)
        slot_grads = scaled_grads[global_pair].astype(jnp.float32)
        hidden, grad_gate, grad_up = swiglu_back(gate_pre[column], up_pre[column], hid_grad[column])
        factor = lax.dynamic_slice_in_dim(proj_hidden, (column_half * FC).astype(jnp.int32), FC, 0)
        blocks = []
        for values, partner in ((hidden, slot_grads), (grad_gate, slot_inputs), (grad_up, slot_inputs)):
            rounded = jnp.dot(values, factor, preferred_element_type=jnp.float32).astype(jnp.bfloat16)
            projected = lax.optimization_barrier(rounded).astype(jnp.float32)
            weighted = member[:, :, None] * partner[:, None, :]
            blocks.append(jnp.einsum("ra,rib->iab", projected, weighted))
        return jnp.stack(blocks, axis=1).reshape(NEX, SKETCH)

    partial_value = lax.map(one_column, jnp.arange(EXPERTS * HALVES, dtype=jnp.int32))
    sketch = jnp.sum(partial_value.reshape(EXPERTS, HALVES, NEX, SKETCH), axis=1).astype(jnp.bfloat16)
    validation = val_sketch.reshape(VAL, EXPERTS, SKETCH).astype(jnp.float32)
    return jnp.einsum("enf,vef->nv", sketch.astype(jnp.float32), validation)
```

```python
import functools

import jax
import jax.numpy as jnp
from jax import lax
from jax.experimental import pallas as pl
from jax.experimental.pallas import tpu as pltpu
from jax.sharding import PartitionSpec as P

HALVES = 2
LANES = 128
CHUNK = 512
TILE = 32
NT = (((1,), (1,)), ((), ()))
TN = (((0,), (0,)), ((), ()))
MESH = pl.DeviceIdType.MESH
F32 = jnp.float32
BF16 = jnp.bfloat16


def dot(a, b, dims=(((1,), (0,)), ((), ()))):
    return lax.dot_general(a, b, dims, preferred_element_type=F32)


def elementwise(gate, up, grad):
    gate = gate.astype(F32)
    up = up.astype(F32)
    grad = grad.astype(F32)
    sig = 0.5 * jnp.tanh(0.5 * gate) + 0.5
    silu = gate * sig
    slope = sig + silu * (1.0 - sig)
    return (
        (silu * up).astype(BF16),
        (grad * up * slope).astype(BF16),
        (grad * silu).astype(BF16),
    )


def kernel(
    peers, capacity, cap_rows,
    tokens, out_grad, routes, weights, gate, up, grad, model_t, hidden_t, val,
    out,
    tok_v, og_v, routes_v, weights_v, gate_v, up_v, grad_v, model_v, hidden_v, val_v,
    factor_v, act, acc, send_rows, recv_rows, part, part_send, part_recv, both, score_send, score_recv,
    load_sem, chunk_sem, row_send, row_recv, part_ssem, part_rsem, score_ssem, score_rsem,
):
    experts = peers // HALVES
    me = lax.axis_index("expert")
    core = lax.axis_index("dp")
    column = lax.rem(me, HALVES)
    partner = me + 1 - 2 * column
    tok_rows, k = tok_v.shape[0], model_v.shape[0]
    slot_rows, width = gate_v.shape
    chunks = width // CHUNK

    block = pl.ds(pl.multiple_of((me * 2 + core) * tok_rows, tok_rows), tok_rows)
    columns = pl.ds(pl.multiple_of(column * width, LANES), width)
    loads = [
        pltpu.make_async_copy(src, dst, load_sem.at[i])
        for i, (src, dst) in enumerate(
            (
                (routes.at[:, block], routes_v),
                (weights.at[:, block], weights_v),
                (model_t, model_v),
                (tokens, tok_v),
                (out_grad, og_v),
                (hidden_t.at[:, columns], hidden_v),
                (val, val_v),
            )
        )
    ]
    streams = [
        [
            pltpu.make_async_copy(
                src.at[0, :, pl.ds(c * CHUNK, CHUNK)],
                dst.at[:, pl.ds(c * CHUNK, CHUNK)],
                chunk_sem.at[i, c],
            )
            for i, (src, dst) in enumerate(((gate, gate_v), (up, up_v), (grad, grad_v)))
        ]
        for c in range(chunks)
    ]
    for copy in loads[:6]:
        copy.start()
    for group in streams:
        for copy in group:
            copy.start()
    loads[6].start()

    barrier = pltpu.get_barrier_semaphore()
    for d in range(1, peers):
        pl.semaphore_signal(
            barrier, inc=1, device_id={"expert": lax.rem(me + d, peers)}, device_id_type=MESH
        )
    pl.semaphore_signal(barrier, inc=1, device_id={"dp": 1 - core}, device_id_type=MESH)
    pl.semaphore_signal(
        barrier, inc=1, device_id={"expert": partner, "dp": 1 - core}, device_id_type=MESH
    )

    for copy in loads[:5]:
        copy.wait()
    proj = jnp.concatenate(
        [dot(tok_v[...], model_v[...], NT), dot(og_v[...], model_v[...], NT)], axis=1
    )
    lane = lax.broadcasted_iota(jnp.int32, (tok_rows, 2 * k), 1)
    high = proj.astype(BF16)
    low = jnp.where(lane < k, 0.0, proj - high.astype(F32)).astype(BF16)
    table = jnp.concatenate([high, low], axis=1)
    ids = lax.broadcasted_iota(jnp.int32, (experts, tok_rows), 0)
    first = routes_v[0:1, :] == ids
    second = routes_v[1:2, :] == ids
    named = jnp.where(first | second, 1.0, 0.0).astype(F32)
    row_weight = jnp.where(first, weights_v[0:1, :], jnp.where(second, weights_v[1:2, :], 0.0))
    square = (tok_rows, tok_rows)
    earlier = jnp.where(
        lax.broadcasted_iota(jnp.int32, square, 0) < lax.broadcasted_iota(jnp.int32, square, 1),
        1.0,
        0.0,
    ).astype(BF16)
    rank = dot(named.astype(BF16), earlier).astype(jnp.int32)
    slot = lax.broadcasted_iota(jnp.int32, (cap_rows, tok_rows), 0)
    slot_lane = lax.broadcasted_iota(jnp.int32, (cap_rows, 2 * k), 1)
    for e in range(experts):
        chosen = jnp.where(
            (rank[e : e + 1, :] == slot) & (slot < capacity), named[e : e + 1, :], 0.0
        )
        slot_weight = jnp.sum(chosen * row_weight[e : e + 1, :], axis=1, keepdims=True)
        picked = dot(chosen.astype(BF16), table)
        rows = picked[:, : 2 * k] + picked[:, 2 * k :]
        send_rows[e] = jnp.where(slot_lane < k, rows, rows * slot_weight).astype(BF16)
    pl.semaphore_wait(barrier, peers + 1)
    row_copies = []
    for d in range(1, peers):
        target = lax.rem(me + d, peers)
        copy = pltpu.make_async_remote_copy(
            src_ref=send_rows.at[target // HALVES],
            dst_ref=recv_rows.at[me],
            send_sem=row_send.at[d - 1],
            recv_sem=row_recv.at[d - 1],
            device_id={"expert": target},
            device_id_type=MESH,
        )
        copy.start()
        row_copies.append(copy)
    recv_rows[me] = send_rows[me // HALVES]

    loads[5].wait()
    shape = (k, k)
    to, source = (lax.broadcasted_iota(jnp.int32, shape, axis) for axis in (0, 1))
    order = jnp.where(source == jnp.where(to < k // 2, 2 * to, 2 * to - k + 1), 1.0, 0.0)
    order = order.astype(BF16)
    for c in range(chunks):
        here = pl.ds(c * CHUNK, CHUNK)
        factor_v[:, here] = dot(order, hidden_v[:, here]).astype(BF16)

    def multiply(c):
        here = pl.ds(c * CHUNK, CHUNK)
        value = dot(act[c % 2], factor_v[:, here], NT)
        if c == 0:
            acc[...] = value
        else:
            acc[...] += value

    for c in range(chunks):
        for copy in streams[c]:
            copy.wait()
        here = pl.ds(c * CHUNK, CHUNK)
        for t in range(slot_rows // TILE):
            rows = pl.ds(t * TILE, TILE)
            values = elementwise(gate_v[rows, here], up_v[rows, here], grad_v[rows, here])
            for i, value in enumerate(values):
                act[c % 2, pl.ds(i * slot_rows + t * TILE, TILE), :] = value
        if c > 0:
            multiply(c - 1)
    multiply(chunks - 1)

    for copy in row_copies:
        copy.wait()
    pairs = recv_rows[...].reshape(peers * cap_rows, 2 * k)
    if cap_rows != capacity:
        grid = (slot_rows, peers * cap_rows)
        row, col = (lax.broadcasted_iota(jnp.int32, grid, axis) for axis in (0, 1))
        spot = (row // capacity) * cap_rows + row % capacity
        pairs = dot(jnp.where(col == spot, 1.0, 0.0).astype(BF16), pairs).astype(BF16)
    half = k // 2
    half_lane = lax.broadcasted_iota(jnp.int32, (half, 2 * k), 1)
    blocks = []
    for i in range(3):
        sketch = acc[pl.ds(i * slot_rows, slot_rows), :].astype(BF16)
        outer = dot(sketch, pairs, TN)
        even, odd = outer[:half], outer[half:]
        if i == 0:
            even = pltpu.roll(even, k, 1)
        else:
            odd = pltpu.roll(odd, k, 1)
        blocks.append(jnp.where(half_lane < k, even, odd))
    whole = jnp.concatenate(blocks, axis=0)
    part_rows = whole.shape[0] // HALVES
    for c in range(HALVES):
        piece = whole[c * part_rows : (c + 1) * part_rows]
        part[c] = piece
        part_send[c] = piece.astype(BF16)
    part_copies = []
    for i, (which, device) in enumerate(
        (
            (1 - column, {"expert": partner}),
            (1 - column, {"expert": partner, "dp": 1 - core}),
            (column, {"dp": 1 - core}),
        )
    ):
        copy = pltpu.make_async_remote_copy(
            src_ref=part_send.at[which],
            dst_ref=part_recv.at[i],
            send_sem=part_ssem.at[i],
            recv_sem=part_rsem.at[i],
            device_id=device,
            device_id_type=MESH,
        )
        copy.start()
        part_copies.append(copy)
    loads[6].wait()
    for copy in part_copies:
        copy.wait()
    own = part[column] + part_recv[0].astype(F32)
    other = part_recv[1].astype(F32) + part_recv[2].astype(F32)
    both[0] = jnp.where(core == 0, own, other)
    both[1] = jnp.where(core == 0, other, own)
    totals = [jnp.zeros((val_v.shape[0], LANES), F32) for _ in range(2)]
    for i in range(part_rows):
        values = val_v[:, pl.ds(i * LANES, LANES)].astype(F32)
        for n in range(2):
            totals[n] = totals[n] + values * both[n, pl.ds(i, 1), :]
    scores = jnp.sum(jnp.concatenate(totals, axis=0).T, axis=0, keepdims=True)
    score_send[...] = jnp.broadcast_to(scores, score_send.shape)
    score_copies = []
    for d in range(1, peers):
        copy = pltpu.make_async_remote_copy(
            src_ref=score_send,
            dst_ref=score_recv.at[d - 1],
            send_sem=score_ssem.at[d - 1],
            recv_sem=score_rsem.at[d - 1],
            device_id={"expert": lax.rem(me + d, peers)},
            device_id_type=MESH,
        )
        copy.start()
        score_copies.append(copy)
    for copy in score_copies:
        copy.wait()
    total = score_send[...]
    for d in range(1, peers):
        total = total + score_recv[d - 1]
    count = val_v.shape[0]
    out[0:1, :] = total[0:1, :count]
    out[1:2, :] = total[0:1, count : 2 * count]


def shards(
    tokens, out_grad, routes, route_weight, gate_pre, up_pre, hid_grad, proj_model, proj_hidden, val_sketch
):
    peers = lax.axis_size("expert")
    tok_rows, model = tokens.shape
    _, slot_rows, width = gate_pre.shape
    k = proj_model.shape[1]
    capacity = slot_rows // peers
    cap_rows = -(-capacity // 16) * 16
    val_rows, entries = val_sketch.shape
    part_rows = entries // LANES
    chunks = width // CHUNK
    experts = peers // HALVES
    vmem, dma = pltpu.VMEM, pltpu.SemaphoreType.DMA
    return pl.pallas_call(
        functools.partial(kernel, peers, capacity, cap_rows),
        out_shape=jax.ShapeDtypeStruct((2, val_rows), F32),
        in_specs=[pl.BlockSpec(memory_space=pltpu.HBM)] * 10,
        out_specs=pl.BlockSpec(memory_space=pltpu.VMEM),
        scratch_shapes=[
            vmem((tok_rows, model), BF16),
            vmem((tok_rows, model), BF16),
            vmem((2, tok_rows), jnp.int32),
            vmem((2, tok_rows), F32),
            vmem((slot_rows, width), BF16),
            vmem((slot_rows, width), BF16),
            vmem((slot_rows, width), BF16),
            vmem((k, model), BF16),
            vmem((k, width), BF16),
            vmem((val_rows, entries), BF16),
            vmem((k, width), BF16),
            vmem((2, 3 * slot_rows, CHUNK), BF16),
            vmem((3 * slot_rows, k), F32),
            vmem((experts, cap_rows, 2 * k), BF16),
            vmem((peers, cap_rows, 2 * k), BF16),
            vmem((HALVES, part_rows, LANES), F32),
            vmem((HALVES, part_rows, LANES), BF16),
            vmem((3, part_rows, LANES), BF16),
            vmem((2, part_rows, LANES), F32),
            vmem((8, LANES), F32),
            vmem((peers - 1, 8, LANES), F32),
            dma((7,)),
            dma((3, chunks)),
            dma((peers - 1,)),
            dma((peers - 1,)),
            dma((3,)),
            dma((3,)),
            dma((peers - 1,)),
            dma((peers - 1,)),
        ],
        compiler_params=pltpu.CompilerParams(
            collective_id=0, has_side_effects=True, vmem_limit_bytes=56 * 2**20
        ),
        cost_estimate=pl.CostEstimate(
            flops=2 * 3 * slot_rows * width * k, bytes_accessed=12 * 2**20, transcendentals=slot_rows * width
        ),
    )(
        tokens, out_grad, routes.T, route_weight.T, gate_pre, up_pre, hid_grad,
        proj_model.T, proj_hidden.T, val_sketch,
    )


def solution(mesh):
    return jax.shard_map(
        shards,
        mesh=mesh,
        in_specs=(
            P(("group", "expert", "dp"), None),
            P(("group", "expert", "dp"), None),
            P("group", None),
            P("group", None),
            P("expert", ("group", "dp"), None),
            P("expert", ("group", "dp"), None),
            P("expert", ("group", "dp"), None),
            P(),
            P(),
            P("dp", "expert"),
        ),
        out_specs=P("group", "dp"),
        check_vma=False,
    )
```

```python
import functools

import jax
import jax.numpy as jnp
from jax import lax
from jax.experimental import pallas as pl
from jax.experimental.pallas import tpu as pltpu
from jax.sharding import PartitionSpec as P

HALVES = 2
LANES = 128
CHUNK = 512
TILE = 128
NT = (((1,), (1,)), ((), ()))
TN = (((0,), (0,)), ((), ()))
MESH = pl.DeviceIdType.MESH
F32 = jnp.float32
BF16 = jnp.bfloat16


def dot(a, b, dims=(((1,), (0,)), ((), ()))):
    return lax.dot_general(a, b, dims, preferred_element_type=F32)


def elementwise(gate, up, grad):
    gate = gate.astype(F32)
    sig = 0.5 * jnp.tanh(0.5 * gate) + 0.5
    silu = gate * sig
    slope = sig + silu * (1.0 - sig)
    up = up.astype(F32)
    grad = grad.astype(F32)
    return (
        (silu * up).astype(BF16),
        (grad * up * slope).astype(BF16),
        (grad * silu).astype(BF16),
    )


def kernel(
    peers, capacity, cap_rows,
    tokens, out_grad, routes, weights, gate, up, grad, model_t, hidden_t, val,
    out,
    tok_v, og_v, routes_v, weights_v, gate_v, up_v, grad_v, model_v, hidden_v, val_v,
    factor_v, acc, send_rows, recv_rows, part, part_send, part_recv, both, score_send, score_recv,
    load_sem, chunk_sem, row_send, row_recv, part_ssem, part_rsem, score_ssem, score_rsem,
):
    experts = peers // HALVES
    me = lax.axis_index("expert")
    core = lax.axis_index("dp")
    column = lax.rem(me, HALVES)
    partner = me + 1 - 2 * column
    tok_rows, k = tok_v.shape[0], model_v.shape[0]
    slot_rows, width = gate_v.shape
    chunks = width // CHUNK

    block = pl.ds(pl.multiple_of((me * 2 + core) * tok_rows, tok_rows), tok_rows)
    columns = pl.ds(pl.multiple_of(column * width, LANES), width)
    loads = [
        pltpu.make_async_copy(src, dst, load_sem.at[i])
        for i, (src, dst) in enumerate(
            (
                (routes.at[:, block], routes_v),
                (weights.at[:, block], weights_v),
                (model_t, model_v),
                (tokens, tok_v),
                (out_grad, og_v),
                (hidden_t.at[:, columns], hidden_v),
                (val, val_v),
            )
        )
    ]
    streams = [
        [
            pltpu.make_async_copy(
                src.at[0, :, pl.ds(c * CHUNK, CHUNK)],
                dst.at[:, pl.ds(c * CHUNK, CHUNK)],
                chunk_sem.at[i, c],
            )
            for i, (src, dst) in enumerate(((gate, gate_v), (up, up_v), (grad, grad_v)))
        ]
        for c in range(chunks)
    ]
    for copy in loads[:6]:
        copy.start()
    for group in streams:
        for copy in group:
            copy.start()
    loads[6].start()

    barrier = pltpu.get_barrier_semaphore()
    for d in range(1, peers):
        pl.semaphore_signal(
            barrier, inc=1, device_id={"expert": lax.rem(me + d, peers)}, device_id_type=MESH
        )
    pl.semaphore_signal(barrier, inc=1, device_id={"dp": 1 - core}, device_id_type=MESH)
    pl.semaphore_signal(
        barrier, inc=1, device_id={"expert": partner, "dp": 1 - core}, device_id_type=MESH
    )

    for copy in loads[:5]:
        copy.wait()
    proj = jnp.concatenate(
        [dot(tok_v[...], model_v[...], NT), dot(og_v[...], model_v[...], NT)], axis=1
    )
    lane = lax.broadcasted_iota(jnp.int32, (tok_rows, 2 * k), 1)
    high = proj.astype(BF16)
    low = jnp.where(lane < k, 0.0, proj - high.astype(F32)).astype(BF16)
    table = jnp.concatenate([high, low], axis=1)
    ids = lax.broadcasted_iota(jnp.int32, (experts, tok_rows), 0)
    first = routes_v[0:1, :] == ids
    second = routes_v[1:2, :] == ids
    named = jnp.where(first | second, 1.0, 0.0).astype(F32)
    row_weight = jnp.where(first, weights_v[0:1, :], jnp.where(second, weights_v[1:2, :], 0.0))
    square = (tok_rows, tok_rows)
    earlier = jnp.where(
        lax.broadcasted_iota(jnp.int32, square, 0) < lax.broadcasted_iota(jnp.int32, square, 1),
        1.0,
        0.0,
    ).astype(BF16)
    rank = dot(named.astype(BF16), earlier).astype(jnp.int32)
    slot = lax.broadcasted_iota(jnp.int32, (cap_rows, tok_rows), 0)
    slot_lane = lax.broadcasted_iota(jnp.int32, (cap_rows, 2 * k), 1)
    for e in range(experts):
        chosen = jnp.where(
            (rank[e : e + 1, :] == slot) & (slot < capacity), named[e : e + 1, :], 0.0
        )
        slot_weight = jnp.sum(chosen * row_weight[e : e + 1, :], axis=1, keepdims=True)
        picked = dot(chosen.astype(BF16), table)
        rows = picked[:, : 2 * k] + picked[:, 2 * k :]
        send_rows[e] = jnp.where(slot_lane < k, rows, rows * slot_weight).astype(BF16)
    pl.semaphore_wait(barrier, peers + 1)
    row_copies = []
    for d in range(1, peers):
        target = lax.rem(me + d, peers)
        copy = pltpu.make_async_remote_copy(
            src_ref=send_rows.at[target // HALVES],
            dst_ref=recv_rows.at[me],
            send_sem=row_send.at[d - 1],
            recv_sem=row_recv.at[d - 1],
            device_id={"expert": target},
            device_id_type=MESH,
        )
        copy.start()
        row_copies.append(copy)
    recv_rows[me] = send_rows[me // HALVES]

    loads[5].wait()
    shape = (k, k)
    to, source = (lax.broadcasted_iota(jnp.int32, shape, axis) for axis in (0, 1))
    order = jnp.where(source == jnp.where(to < k // 2, 2 * to, 2 * to - k + 1), 1.0, 0.0)
    order = order.astype(BF16)
    for c in range(chunks):
        here = pl.ds(c * CHUNK, CHUNK)
        factor_v[here, :] = dot(hidden_v[:, here], order, (((0,), (1,)), ((), ()))).astype(BF16)

    for c in range(chunks):
        for copy in streams[c]:
            copy.wait()
        here = pl.ds(c * CHUNK, CHUNK)
        for t in range(slot_rows // TILE):
            rows = pl.ds(t * TILE, TILE)
            values = elementwise(gate_v[rows, here], up_v[rows, here], grad_v[rows, here])
            product = dot(jnp.concatenate(values, axis=0), factor_v[here, :])
            for i in range(3):
                piece = product[i * TILE : (i + 1) * TILE]
                spot = pl.ds(i * slot_rows + t * TILE, TILE)
                acc[spot, :] = piece if c == 0 else acc[spot, :] + piece

    for copy in row_copies:
        copy.wait()
    pairs = recv_rows[...].reshape(peers * cap_rows, 2 * k)
    if cap_rows != capacity:
        grid = (slot_rows, peers * cap_rows)
        row, col = (lax.broadcasted_iota(jnp.int32, grid, axis) for axis in (0, 1))
        spot = (row // capacity) * cap_rows + row % capacity
        pairs = dot(jnp.where(col == spot, 1.0, 0.0).astype(BF16), pairs).astype(BF16)
    half = k // 2
    half_lane = lax.broadcasted_iota(jnp.int32, (half, 2 * k), 1)
    blocks = []
    for i in range(3):
        sketch = acc[pl.ds(i * slot_rows, slot_rows), :].astype(BF16)
        outer = dot(sketch, pairs, TN)
        even, odd = outer[:half], outer[half:]
        if i == 0:
            even = pltpu.roll(even, k, 1)
        else:
            odd = pltpu.roll(odd, k, 1)
        blocks.append(jnp.where(half_lane < k, even, odd))
    whole = jnp.concatenate(blocks, axis=0)
    part_rows = whole.shape[0] // HALVES
    for c in range(HALVES):
        piece = whole[c * part_rows : (c + 1) * part_rows]
        part[c] = piece
        part_send[c] = piece.astype(BF16)
    part_copies = []
    for i, (which, device) in enumerate(
        (
            (1 - column, {"expert": partner}),
            (1 - column, {"expert": partner, "dp": 1 - core}),
            (column, {"dp": 1 - core}),
        )
    ):
        copy = pltpu.make_async_remote_copy(
            src_ref=part_send.at[which],
            dst_ref=part_recv.at[i],
            send_sem=part_ssem.at[i],
            recv_sem=part_rsem.at[i],
            device_id=device,
            device_id_type=MESH,
        )
        copy.start()
        part_copies.append(copy)
    loads[6].wait()
    for copy in part_copies:
        copy.wait()
    own = part[column] + part_recv[0].astype(F32)
    other = part_recv[1].astype(F32) + part_recv[2].astype(F32)
    both[0] = jnp.where(core == 0, own, other)
    both[1] = jnp.where(core == 0, other, own)
    totals = [jnp.zeros((val_v.shape[0], LANES), F32) for _ in range(2)]
    for i in range(part_rows):
        values = val_v[:, pl.ds(i * LANES, LANES)].astype(F32)
        for n in range(2):
            totals[n] = totals[n] + values * both[n, pl.ds(i, 1), :]
    scores = jnp.sum(jnp.concatenate(totals, axis=0).T, axis=0, keepdims=True)
    score_send[...] = jnp.broadcast_to(scores, score_send.shape)
    score_copies = []
    for d in range(1, peers):
        copy = pltpu.make_async_remote_copy(
            src_ref=score_send,
            dst_ref=score_recv.at[d - 1],
            send_sem=score_ssem.at[d - 1],
            recv_sem=score_rsem.at[d - 1],
            device_id={"expert": lax.rem(me + d, peers)},
            device_id_type=MESH,
        )
        copy.start()
        score_copies.append(copy)
    for copy in score_copies:
        copy.wait()
    total = score_send[...]
    for d in range(1, peers):
        total = total + score_recv[d - 1]
    count = val_v.shape[0]
    out[0:1, :] = total[0:1, :count]
    out[1:2, :] = total[0:1, count : 2 * count]


def shards(
    tokens, out_grad, routes, route_weight, gate_pre, up_pre, hid_grad, proj_model, proj_hidden, val_sketch
):
    peers = lax.axis_size("expert")
    tok_rows, model = tokens.shape
    _, slot_rows, width = gate_pre.shape
    k = proj_model.shape[1]
    capacity = slot_rows // peers
    cap_rows = -(-capacity // 16) * 16
    val_rows, entries = val_sketch.shape
    part_rows = entries // LANES
    chunks = width // CHUNK
    experts = peers // HALVES
    vmem, dma = pltpu.VMEM, pltpu.SemaphoreType.DMA
    return pl.pallas_call(
        functools.partial(kernel, peers, capacity, cap_rows),
        out_shape=jax.ShapeDtypeStruct((2, val_rows), F32),
        in_specs=[pl.BlockSpec(memory_space=pltpu.HBM)] * 10,
        out_specs=pl.BlockSpec(memory_space=pltpu.VMEM),
        scratch_shapes=[
            vmem((tok_rows, model), BF16),
            vmem((tok_rows, model), BF16),
            vmem((2, tok_rows), jnp.int32),
            vmem((2, tok_rows), F32),
            vmem((slot_rows, width), BF16),
            vmem((slot_rows, width), BF16),
            vmem((slot_rows, width), BF16),
            vmem((k, model), BF16),
            vmem((k, width), BF16),
            vmem((val_rows, entries), BF16),
            vmem((width, k), BF16),
            vmem((3 * slot_rows, k), F32),
            vmem((experts, cap_rows, 2 * k), BF16),
            vmem((peers, cap_rows, 2 * k), BF16),
            vmem((HALVES, part_rows, LANES), F32),
            vmem((HALVES, part_rows, LANES), BF16),
            vmem((3, part_rows, LANES), BF16),
            vmem((2, part_rows, LANES), F32),
            vmem((8, LANES), F32),
            vmem((peers - 1, 8, LANES), F32),
            dma((7,)),
            dma((3, chunks)),
            dma((peers - 1,)),
            dma((peers - 1,)),
            dma((3,)),
            dma((3,)),
            dma((peers - 1,)),
            dma((peers - 1,)),
        ],
        compiler_params=pltpu.CompilerParams(
            collective_id=0, has_side_effects=True, vmem_limit_bytes=56 * 2**20
        ),
        cost_estimate=pl.CostEstimate(
            flops=2 * 3 * slot_rows * width * k, bytes_accessed=12 * 2**20, transcendentals=slot_rows * width
        ),
    )(
        tokens, out_grad, routes.T, route_weight.T, gate_pre, up_pre, hid_grad,
        proj_model.T, proj_hidden.T, val_sketch,
    )


def solution(mesh):
    return jax.shard_map(
        shards,
        mesh=mesh,
        in_specs=(
            P(("group", "expert", "dp"), None),
            P(("group", "expert", "dp"), None),
            P("group", None),
            P("group", None),
            P("expert", ("group", "dp"), None),
            P("expert", ("group", "dp"), None),
            P("expert", ("group", "dp"), None),
            P(),
            P(),
            P("dp", "expert"),
        ),
        out_specs=P("group", "dp"),
        check_vma=False,
    )
```
